768 devices in a mesh: dp: 32 (over y_lo, x, core), expert: 24 (over y_hi, z).
Axes of the slice: x: 4, y: 8 (y_hi: 2, y_lo: 4; y = y_hi * 4 + y_lo), z: 12, core: 2. Of those that a mesh axis runs over, the one named last changes fastest.
Arguments:
- frames: bfloat16 [4096, 1536], P('dp', 'expert'), may hold values from -6 to 6
- cotangent: bfloat16 [4096, 1536], P('dp', 'expert'), may hold values from -6 to 6
- routes: int32 [4096, 2], P('dp'), may hold values from 0 to 23, all different within a row; in each aligned block of 128 rows (0 to 127, 128 to 255, ...) at most 16 rows name the same one
- route_gates: float32 [4096, 2], P('dp'), may hold values from 0.25 to 1
- norm_gain: float32 [1536], replicated, may hold values from 0.1 to 1.9
- norm_bias: float32 [1536], replicated, may hold values from -3 to 3
- expert_in: bfloat16 [24, 1536, 6144], P('expert', None, 'dp'), may hold values from -0.15625 to 0.15625
- expert_out: bfloat16 [24, 6144, 1536], P('expert', 'dp'), may hold values from -0.078125 to 0.078125
Outputs:
- output: bfloat16 [4096, 1536], P('dp', 'expert')
- frame_grads: bfloat16 [4096, 1536], P('dp', 'expert')
- grad_in: float32 [24, 1536, 6144], P('expert', None, 'dp')
- grad_out: float32 [24, 6144, 1536], P('expert', 'dp')
The draws below stay inside these ranges and needn't reach their ends.
Inputs may be any that keep to these rules, and one draw needn't show every extreme that they name: `routes`: each frame names two different experts. Within each aligned block of 128 frames no expert is named more than 16 times, a bound that some block reaches.
All inputs are finite; a program needn't handle non-finite values.
Results may differ from the reference program's by a relative error of at most 0.015.
Values may be sent and summed in bfloat16 or wider, within the bound.
No kernel may reach another device: no remote copies, remote signals or barrier semaphores. Data moves between devices by JAX's collectives and lax.ppermute only.
A program may use at most 64 MiB of HBM per device.

```python
import math
import jax
import jax.numpy as jnp
import numpy as np
from jax import lax

D = 1536
FF = 6144
TOK_DP = 128
EXPERTS = 24
CAP = 16
TOKENS = 4096
N_DP = 32


def steps_of(own_key, dims, cuts, smallest, largest):
    loudness, own = 1.0, jax.random.fold_in(own_key, 6)
    for dim, blocks in cuts:
        draws = jnp.exp(jax.random.uniform(jax.random.fold_in(own, dim), (blocks,), jnp.float32, smallest / len(cuts), largest / len(cuts)))
        loudness = loudness * jnp.repeat(draws, dims[dim] // blocks).reshape([-1 if axis == dim else 1 for axis in range(len(dims))])
    return loudness


def deal_out(key, own, number, rows, number_of, top, limit, skew):
    sequence = jax.random.permutation(key, number_of)
    heavy_load, usual = load_shares(number_of, rows * top, limit, skew, True), load_shares(number_of, rows * top, limit, skew, False)
    places = jnp.arange(number_of)

    def named(sizes, offset_by):
        used = int((sizes > 0).sum())
        fixed = max(1, used // 4)
        shifted = fixed + (places - fixed + offset_by * (used - fixed)) % max(1, number_of - fixed)
        return jnp.zeros((number_of,), jnp.int32).at[sequence[jnp.where(places < fixed, places, shifted)]].set(jnp.asarray(sizes, jnp.int32))

    sizes = jnp.where(number % 4 == 0, named(heavy_load, number // 4), named(usual, number - number // 4 - 1))
    mixed = jax.random.permutation(jax.random.fold_in(own, 3), number_of)
    giver, receiver = mixed[0:number_of // 2 * 2:2], mixed[1:number_of // 2 * 2:2]
    margin = jnp.minimum(sizes[giver] - 1, limit - sizes[receiver]) // 2
    margin = jnp.where((giver == sequence[0]) | (receiver == sequence[0]) | (sizes[receiver] == 0), 0, jnp.maximum(margin, 0))
    shifted = jax.random.randint(jax.random.fold_in(own, 4), (number_of // 2,), 0, 1 << 20) % (margin + 1)
    sizes = sizes.at[giver].add(-shifted).at[receiver].add(shifted)
    members = jnp.searchsorted(jnp.cumsum(sizes), jnp.arange(rows * top), side="right").astype(jnp.int32)
    table = members.reshape(top, rows).T
    table = table[jax.random.permutation(jax.random.fold_in(own, 1), rows)]
    offset_by = jax.random.randint(jax.random.fold_in(own, 2), (rows, 1), 0, top)
    return jnp.take_along_axis(table, (jnp.arange(top)[None, :] + offset_by) % top, axis=1)


def load_shares(count, total, limit, skew, full):
    portions = [(1 << 20) // math.isqrt(grade ** skew) + 1 for grade in range(1, count + 1)]
    largest = limit if full else min(limit, max(-(-total // count), total * portions[0] // sum(portions)))
    least = 1 if total - largest >= count - 1 else 0
    holding, surplus = [largest] + [least] * (count - 1), total - largest - least * (count - 1)
    while surplus > 0:
        movable = [i for i in range(1, count) if holding[i] < largest] or [i for i in range(1, count) if holding[i] < limit]
        whole, left = sum([portions[i] for i in movable]), surplus
        for i in movable:
            more = min(limit - holding[i], max(1, left * portions[i] // whole), surplus)
            holding[i] = holding[i] + more
            surplus = surplus - more
    return np.array(holding)


def noise(key, shape, spread, bound, shards=(), held_as=jnp.bfloat16):
    values = spread * jax.random.normal(key, shape, jnp.float32)
    if shards:
        values = values * steps_of(key, shape, shards, -0.22, 0.18)
    return jnp.clip(values, -bound, bound).astype(held_as)


def setup_inputs(seed: int = 0) -> dict:
    splits = jax.random.split(jax.random.key(seed), 9)
    frames = noise(splits[0], (TOKENS, D), 1.0, 6.0, ((0, 32), (1, 24)))
    cotangent = noise(splits[1], (TOKENS, D), 1.0, 6.0, ((0, 32), (1, 24)))
    routes_keys = jax.random.split(jax.random.fold_in(splits[2], 1), TOKENS // TOK_DP)
    routes_turns = jax.random.permutation(jax.random.fold_in(splits[2], 3), TOKENS // TOK_DP)
    routes = jax.vmap(lambda own, number: deal_out(jax.random.fold_in(splits[2], 2), own, number, TOK_DP, EXPERTS, 2, CAP, 2))(routes_keys, routes_turns).reshape((TOKENS, 2))
    route_gates = jnp.clip(0.25 + 0.75 * jax.random.uniform(splits[3], (TOKENS, 2), jnp.float32) ** steps_of(splits[3], (TOKENS, 2), ((0, 32),), -0.2, 0.2), 0.25, 1.0)
    norm_gain = jnp.clip(1.0 + 0.18 * jax.random.normal(splits[4], (D,), jnp.float32), 0.1, 1.9)
    norm_bias = noise(splits[5], (D,), 0.5, 3.0, (), jnp.float32)
    expert_in = noise(splits[6], (EXPERTS, D, FF), D ** -0.5, 0.15625, ((0, 24), (2, 32)))
    expert_out = noise(splits[7], (EXPERTS, FF, D), FF ** -0.5, 0.078125, ((0, 24), (1, 32)))
    return dict(frames=frames, cotangent=cotangent, routes=routes, route_gates=route_gates, norm_gain=norm_gain, norm_bias=norm_bias, expert_in=expert_in, expert_out=expert_out)


epsilon = 1e-05

def normalize(rows, norm_gain, norm_bias):
    values = rows.astype(jnp.float32)
    row_mean = lax.optimization_barrier(jnp.mean(values, axis=-1, keepdims=True))
    centered = values - row_mean
    row_var = lax.optimization_barrier(jnp.mean(centered * centered, axis=-1, keepdims=True))
    scaled = lax.rsqrt(row_var + epsilon)
    unit = centered * scaled
    normed = (unit * norm_gain + norm_bias).astype(jnp.bfloat16)
    return (normed, unit, scaled)

def group_sum(left, right):
    rows = left.shape[0]
    width = right.shape[-1]
    group = FF // N_DP
    left_groups = left.reshape(rows, N_DP, group).astype(jnp.float32)
    right_groups = right.reshape(N_DP, group, width).astype(jnp.float32)

    def add_group(total, index):
        piece = lax.dynamic_index_in_dim(left_groups, index, 1, keepdims=False)
        weight = lax.dynamic_index_in_dim(right_groups, index, 0, keepdims=False)
        part = jnp.dot(piece, weight).astype(jnp.bfloat16)
        return (total + lax.optimization_barrier(part).astype(jnp.float32), None)
    total, unused = lax.scan(add_group, jnp.zeros((rows, width), jnp.float32), jnp.arange(N_DP, dtype=jnp.int32))
    return total

def expert_block(rows, grads, weight_in, weight_out, norm_gain, norm_bias):
    normed, unit, scaled = normalize(rows, norm_gain, norm_bias)
    inner = jnp.dot(normed, weight_in, preferred_element_type=jnp.float32)
    hidden = jax.nn.silu(inner).astype(jnp.bfloat16)
    result = group_sum(hidden, weight_out).astype(jnp.bfloat16)
    back_hidden = jnp.dot(grads, weight_out.T, preferred_element_type=jnp.float32)
    sigm = jax.nn.sigmoid(inner)
    back_inner = (back_hidden * sigm * (1.0 + inner * (1.0 - sigm))).astype(jnp.bfloat16)
    grad_out = jnp.dot(hidden.T, grads, preferred_element_type=jnp.float32)
    grad_in = jnp.dot(normed.T, back_inner, preferred_element_type=jnp.float32)
    back_normed = group_sum(back_inner, weight_in.T)
    back_unit = back_normed * norm_gain
    first = lax.optimization_barrier(jnp.mean(back_unit, axis=-1, keepdims=True))
    second = lax.optimization_barrier(jnp.mean(back_unit * unit, axis=-1, keepdims=True))
    back_rows = ((back_unit - first - unit * second) * scaled).astype(jnp.bfloat16)
    return (result, back_rows, grad_in, grad_out)

def reference(frames, cotangent, routes, route_gates, norm_gain, norm_bias, expert_in, expert_out):
    total = N_DP * TOK_DP * 2
    flat_routes = routes.reshape(N_DP, TOK_DP * 2).astype(jnp.int32)
    onehot = (flat_routes[:, :, None] == jnp.arange(EXPERTS, dtype=jnp.int32)[None, None, :]).astype(jnp.int32)
    earlier = jnp.cumsum(onehot, axis=1) - onehot
    slots = lax.optimization_barrier(jnp.sum(earlier * onehot, axis=-1)).reshape(-1).astype(jnp.int32)
    expert_ids = flat_routes.reshape(-1)
    block_ids = (jnp.arange(total, dtype=jnp.int32) // (TOK_DP * 2)).astype(jnp.int32)
    token_ids = (jnp.arange(total, dtype=jnp.int32) // 2).astype(jnp.int32)
    scales = 0.5 * route_gates.reshape(-1).astype(jnp.float32)
    picked_rows = frames[token_ids]
    picked_grads = (scales[:, None] * cotangent[token_ids].astype(jnp.float32)).astype(jnp.bfloat16)
    buffer_rows = jnp.zeros((EXPERTS, N_DP, CAP, D), jnp.bfloat16).at[expert_ids, block_ids, slots].set(picked_rows)
    buffer_grads = jnp.zeros((EXPERTS, N_DP, CAP, D), jnp.bfloat16).at[expert_ids, block_ids, slots].set(picked_grads)

    def one_expert(items):
        rows, grads, weight_in, weight_out = items
        return expert_block(rows.reshape(N_DP * CAP, D), grads.reshape(N_DP * CAP, D), weight_in, weight_out, norm_gain, norm_bias)
    results, back_rows, grad_in, grad_out = lax.map(one_expert, (buffer_rows, buffer_grads, expert_in, expert_out))
    results = results.reshape(EXPERTS, N_DP, CAP, D)
    back_rows = back_rows.reshape(EXPERTS, N_DP, CAP, D)
    taken = results[expert_ids, block_ids, slots].astype(jnp.float32) * scales[:, None]
    output = (frames.astype(jnp.float32) + lax.optimization_barrier(jnp.sum(taken.reshape(TOKENS, 2, D), axis=1))).astype(jnp.bfloat16)
    taken_back = back_rows[expert_ids, block_ids, slots].astype(jnp.float32)
    frame_grads = (cotangent.astype(jnp.float32) + lax.optimization_barrier(jnp.sum(taken_back.reshape(TOKENS, 2, D), axis=1))).astype(jnp.bfloat16)
    return (output, frame_grads, grad_in, grad_out)
```

```python
import jax
import jax.numpy as jnp
from jax import lax
from jax.experimental import pallas as pl
from jax.experimental.pallas import tpu as pltpu
from jax.sharding import Mesh
from jax.sharding import PartitionSpec as P

epsilon = 1e-05
LANES = 128
HALF = 64
Y_LO, X, CORE, Y_HI, Z = 4, 4, 2, 2, 12
EXPERTS = Y_HI * Z
CAP = 16
SLOTS = EXPERTS * CAP
ROWS = Y_LO * CAP
DP_AXES = ("yl", "x", "core")
EXPERT_AXES = ("yh", "z")
F32 = jnp.float32
BF16 = jnp.bfloat16


def call(kernel, out_shapes, flops=0, bytes_accessed=0):
    return pl.pallas_call(
        kernel,
        out_shape=out_shapes,
        compiler_params=pltpu.CompilerParams(vmem_limit_bytes=40 * 1024 * 1024),
        cost_estimate=pl.CostEstimate(
            flops=flops, bytes_accessed=bytes_accessed, transcendentals=0
        ),
    )


def dot(a, b, ca, cb):
    return lax.dot_general(a, b, (((ca,), (cb,)), ((), ())), preferred_element_type=F32)


def places(routes):
    tokens = routes.shape[1]
    first, second = routes[0:1], routes[1:2]
    experts = lax.broadcasted_iota(jnp.int32, (EXPERTS, tokens), 0)
    names = (experts == first, experts == second)
    either = (names[0] | names[1]).astype(F32)
    before = lax.broadcasted_iota(jnp.int32, (tokens, tokens), 0) < lax.broadcasted_iota(
        jnp.int32, (tokens, tokens), 1
    )
    earlier = dot(either.astype(BF16), before.astype(F32).astype(BF16), 1, 0)
    rows = lax.broadcasted_iota(jnp.int32, (SLOTS, tokens), 0)
    masks = []
    for name, expert in zip(names, (first, second)):
        slot = jnp.sum(jnp.where(name, earlier, 0.0), axis=0, keepdims=True)
        masks.append(rows == expert * CAP + slot.astype(jnp.int32))
    return masks


def route_kernel(routes_ref, gates_ref, frames_ref, cotangent_ref, out_ref):
    mask0, mask1 = places(routes_ref[...])
    gates = 0.5 * gates_ref[...]
    scale = jnp.sum(
        jnp.where(mask0, gates[0:1], 0.0) + jnp.where(mask1, gates[1:2], 0.0),
        axis=1,
        keepdims=True,
    )
    chosen = (mask0 | mask1).astype(F32).astype(BF16)
    both = jnp.concatenate([frames_ref[...], cotangent_ref[...]], axis=0)
    picked = dot(chosen, both, 1, 1)
    lane = lax.broadcasted_iota(jnp.int32, picked.shape, 1)
    sent = jnp.where(lane < HALF, picked, picked * scale).astype(BF16)
    sent = sent.reshape(EXPERTS, CAP, LANES)
    for y in range(Y_LO):
        out_ref[y] = sent


def swap_halves(a):
    return pltpu.roll(a, HALF, 1)


def normal(rows):
    mean = jnp.mean(rows, axis=-1, keepdims=True)
    centered = rows - mean
    var = jnp.mean(centered * centered, axis=-1, keepdims=True)
    scaled = lax.rsqrt(var + epsilon)
    return centered * scaled, scaled


def normalize_kernel(came_ref, gain_ref, bias_ref, sent_ref, rows_ref, values_ref):
    lane = lax.broadcasted_iota(jnp.int32, (ROWS, LANES), 1)
    for p in range(EXPERTS // 2):
        a = came_ref[:, 2 * p].astype(F32).reshape(ROWS, LANES)
        b = came_ref[:, 2 * p + 1].astype(F32).reshape(ROWS, LANES)
        cols = slice(p * LANES, (p + 1) * LANES)
        values_ref[:, cols] = jnp.where(lane < HALF, a, swap_halves(b))
        sent_ref[ROWS:, cols] = jnp.where(lane < HALF, swap_halves(a), b).astype(BF16)
    values = values_ref[...]
    rows_ref[...] = values.astype(BF16)
    unit, _ = normal(values)
    sent_ref[:ROWS] = (unit * gain_ref[...] + bias_ref[...]).astype(BF16)


def expert_kernel(
    x0, x1, x2, x3, in_own, in_sib, out_own, out_sib, p0, p1, p2, p3, hid_ref, back_ref
):
    width = x0.shape[1]
    normed = jnp.concatenate([x[:ROWS] for x in (x0, x1, x2, x3)], axis=0)
    grads = jnp.concatenate([x[ROWS:] for x in (x0, x1, x2, x3)], axis=0)
    weight_in = jnp.concatenate([in_own[...], in_sib[...]], axis=0)
    weight_out = jnp.concatenate([out_own[...], out_sib[...]], axis=0)
    inner = dot(normed, weight_in, 1, 1)
    back_hidden = dot(grads, weight_out, 1, 1)
    sigm = jax.nn.sigmoid(inner)
    hidden = (inner * sigm).astype(BF16)
    back_inner = (back_hidden * sigm * (1.0 + inner * (1.0 - sigm))).astype(BF16)
    hid_ref[...] = hidden
    back_ref[...] = back_inner
    for i, p in enumerate((p0, p1, p2, p3)):
        rows = slice(i * ROWS, (i + 1) * ROWS)
        p[:, :width] = dot(hidden[rows], weight_out, 1, 0).astype(p.dtype)
        p[:, width:] = dot(back_inner[rows], weight_in, 1, 0).astype(p.dtype)


def grads_kernel(x0, x1, x2, x3, hid_ref, back_ref, in_ref, out_ref, sib_ref):
    normed = jnp.concatenate([x[:ROWS] for x in (x0, x1, x2, x3)], axis=0)
    grads = jnp.concatenate([x[ROWS:] for x in (x0, x1, x2, x3)], axis=0)
    half = in_ref.shape[0]
    grad_in = dot(back_ref[...], normed, 0, 0)
    in_ref[...] = grad_in[:half]
    sib_ref[:half] = grad_in[half:].astype(BF16)
    grad_out = dot(hid_ref[...], grads, 0, 0)
    out_ref[...] = grad_out[:half]
    sib_ref[half:] = grad_out[half:].astype(BF16)


def back_kernel(p0, p1, p2, p3, rows_ref, gain_ref, out_ref):
    width = rows_ref.shape[1]

    def total(cols):
        return (
            p0[:, cols].astype(F32)
            + p1[:, cols].astype(F32)
            + p2[:, cols].astype(F32)
            + p3[:, cols].astype(F32)
        )

    unit, scaled = normal(rows_ref[...].astype(F32))
    back_unit = total(slice(width, 2 * width)) * gain_ref[...]
    first = jnp.mean(back_unit, axis=-1, keepdims=True)
    second = jnp.mean(back_unit * unit, axis=-1, keepdims=True)
    back = (back_unit - first - unit * second) * scaled
    lane = lax.broadcasted_iota(jnp.int32, (ROWS, LANES), 1)
    for p in range(EXPERTS // 2):
        cols = slice(p * LANES, (p + 1) * LANES)
        a, b = total(cols), back[:, cols]
        low = jnp.where(lane < HALF, a, swap_halves(b))
        high = jnp.where(lane < HALF, swap_halves(a), b)
        out_ref[:, 2 * p] = low.astype(BF16).reshape(Y_LO, CAP, LANES)
        out_ref[:, 2 * p + 1] = high.astype(BF16).reshape(Y_LO, CAP, LANES)


def combine_kernel(came_ref, routes_ref, gates_ref, frames_ref, cotangent_ref, out_ref, fg_ref):
    total = came_ref[0].astype(F32)
    for y in range(1, Y_LO):
        total = total + came_ref[y].astype(F32)
    came = total.astype(BF16).reshape(SLOTS, LANES)
    gates = 0.5 * gates_ref[...]
    taken = [dot(came, mask.astype(F32).astype(BF16), 0, 0) for mask in places(routes_ref[...])]
    results = taken[0][:HALF] * gates[0:1] + taken[1][:HALF] * gates[1:2]
    backs = taken[0][HALF:] + taken[1][HALF:]
    out_ref[...] = (frames_ref[...].astype(F32) + results).astype(BF16)
    fg_ref[...] = (cotangent_ref[...].astype(F32) + backs).astype(BF16)


def ring(size, step):
    return [(i, (i + step) % size) for i in range(size)]


def body(frames, cotangent, routes, route_gates, norm_gain, norm_bias, expert_in, expert_out):
    width = norm_gain.shape[0]
    units = expert_out.shape[1]
    frames_t, cotangent_t = frames.T, cotangent.T
    routes_t, gates_t = routes.T, route_gates.T
    gain, bias = norm_gain[None], norm_bias[None]
    in_own, out_own = expert_in[0].T, expert_out[0]
    shape = jax.ShapeDtypeStruct
    blocks = shape((Y_LO, EXPERTS, CAP, LANES), BF16)

    def exchange(a):
        a = a.reshape(Y_LO * EXPERTS, CAP, LANES)
        a = lax.all_to_all(a, ("yl",) + EXPERT_AXES, split_axis=0, concat_axis=0, tiled=True)
        return a.reshape(Y_LO, EXPERTS, CAP, LANES)

    in_sib = lax.ppermute(in_own, "core", ring(CORE, 1))
    out_sib = lax.ppermute(out_own, "core", ring(CORE, 1))
    came = exchange(call(route_kernel, blocks)(routes_t, gates_t, frames_t, cotangent_t))
    mine, rows = pl.pallas_call(
        normalize_kernel,
        out_shape=(shape((2 * ROWS, width), BF16), shape((ROWS, width), BF16)),
        scratch_shapes=[pltpu.VMEM((ROWS, width), F32)],
        compiler_params=pltpu.CompilerParams(vmem_limit_bytes=40 * 1024 * 1024),
    )(came, gain, bias)
    all_x = [mine] + [lax.ppermute(mine, "x", ring(X, step)) for step in (1, 3, 2)]
    part = shape((ROWS, 2 * width), BF16)
    kept = shape((X * ROWS, CORE * units), BF16)
    p0, p1, p3, p2, hidden, back_inner = call(
        expert_kernel, (shape((ROWS, 2 * width), F32), part, part, part, kept, kept)
    )(*all_x, in_own, in_sib, out_own, out_sib)
    r1 = lax.ppermute(p1, "x", ring(X, 3))
    r3 = lax.ppermute(p3, "x", ring(X, 1))
    r2 = lax.ppermute(p2, "x", ring(X, 2))
    grad_in, grad_out, for_sib = call(
        grads_kernel,
        (
            shape((units, width), F32),
            shape((units, width), F32),
            shape((2 * units, width), BF16),
        ),
        flops=4 * X * ROWS * CORE * units * width,
        bytes_accessed=8 * units * width * 4,
    )(*all_x, hidden, back_inner)
    from_sib = lax.ppermute(for_sib, "core", ring(CORE, 1)).astype(F32)
    grad_in = grad_in + from_sib[:units]
    grad_out = grad_out + from_sib[units:]
    backs = exchange(call(back_kernel, blocks)(p0, r1, r2, r3, rows, gain))
    token = shape(frames_t.shape, BF16)
    output, frame_grads = call(combine_kernel, (token, token))(
        backs, routes_t, gates_t, frames_t, cotangent_t
    )
    return (output.T, frame_grads.T, grad_in.T[None], grad_out[None])


def solution(mesh):
    fine = Mesh(mesh.devices.reshape(Y_LO, X, CORE, Y_HI, Z), DP_AXES + EXPERT_AXES)
    tokens = P(DP_AXES, EXPERT_AXES)
    weights_in = P(EXPERT_AXES, None, DP_AXES)
    weights_out = P(EXPERT_AXES, DP_AXES, None)
    return jax.shard_map(
        body,
        mesh=fine,
        in_specs=(
            tokens,
            tokens,
            P(DP_AXES, None),
            P(DP_AXES, None),
            P(),
            P(),
            weights_in,
            weights_out,
        ),
        out_specs=(tokens, tokens, weights_in, weights_out),
        check_vma=False,
    )
```

```python
import jax
import jax.numpy as jnp
from jax import lax
from jax.experimental import pallas as pl
from jax.experimental.pallas import tpu as pltpu
from jax.sharding import Mesh
from jax.sharding import PartitionSpec as P

epsilon = 1e-05
LANES = 128
HALF = 64
Y_FAR, Y_NEAR, X_HI, X_LO, CORE, Y_HI, Z = 2, 2, 2, 2, 2, 2, 12
EXPERTS = Y_HI * Z
CAP = 16
SLOTS = EXPERTS * CAP
ROWS = Y_FAR * CAP
GROUP = Y_NEAR * X_HI
DP_AXES = ("yfar", "ynear", "xhi", "xlo", "core")
EXPERT_AXES = ("yh", "z")
SWAP = [(0, 1), (1, 0)]
MIB = 1024 * 1024
F32 = jnp.float32
VMEM, ANY = pltpu.VMEM, pl.ANY
DMA = pltpu.SemaphoreType.DMA
BF16 = jnp.bfloat16


def call(kernel, out_shapes, flops=0, bytes_accessed=0, vmem=6, **more):
    return pl.pallas_call(
        kernel,
        out_shape=out_shapes,
        compiler_params=pltpu.CompilerParams(vmem_limit_bytes=vmem * MIB),
        cost_estimate=pl.CostEstimate(
            flops=flops, bytes_accessed=bytes_accessed, transcendentals=0
        ),
        **more,
    )


def spaces(*names):
    return [pl.BlockSpec(memory_space=name) for name in names]


def dot(a, b, ca, cb):
    return lax.dot_general(a, b, (((ca,), (cb,)), ((), ())), preferred_element_type=F32)


def places(routes):
    tokens = routes.shape[1]
    first, second = routes[0:1], routes[1:2]
    experts = lax.broadcasted_iota(jnp.int32, (EXPERTS, tokens), 0)
    names = (experts == first, experts == second)
    either = (names[0] | names[1]).astype(F32)
    before = lax.broadcasted_iota(jnp.int32, (tokens, tokens), 0) < lax.broadcasted_iota(
        jnp.int32, (tokens, tokens), 1
    )
    earlier = dot(either.astype(BF16), before.astype(F32).astype(BF16), 1, 0)
    rows = lax.broadcasted_iota(jnp.int32, (SLOTS, tokens), 0)
    masks = []
    for name, expert in zip(names, (first, second)):
        slot = jnp.sum(jnp.where(name, earlier, 0.0), axis=0, keepdims=True)
        masks.append(rows == expert * CAP + slot.astype(jnp.int32))
    return masks


def route_kernel(routes_ref, gates_ref, frames_ref, cotangent_ref, out_ref):
    mask0, mask1 = places(routes_ref[...])
    gates = 0.5 * gates_ref[...]
    scale = jnp.sum(
        jnp.where(mask0, gates[0:1], 0.0) + jnp.where(mask1, gates[1:2], 0.0),
        axis=1,
        keepdims=True,
    )
    chosen = (mask0 | mask1).astype(F32).astype(BF16)
    both = jnp.concatenate([frames_ref[...], cotangent_ref[...]], axis=0)
    picked = dot(chosen, both, 1, 1)
    lane = lax.broadcasted_iota(jnp.int32, picked.shape, 1)
    sent = jnp.where(lane < HALF, picked, picked * scale).astype(BF16)
    sent = sent.reshape(EXPERTS, CAP, LANES)
    for y in range(Y_FAR):
        out_ref[y] = sent


def swap_halves(a):
    return pltpu.roll(a, HALF, 1)


def normal(rows):
    mean = jnp.mean(rows, axis=-1, keepdims=True)
    centered = rows - mean
    var = jnp.mean(centered * centered, axis=-1, keepdims=True)
    scaled = lax.rsqrt(var + epsilon)
    return centered * scaled, scaled


def normalize_kernel(came_ref, gain_ref, bias_ref, sent_ref, rows_ref, values_ref):
    lane = lax.broadcasted_iota(jnp.int32, (ROWS, LANES), 1)
    for p in range(EXPERTS // 2):
        a = came_ref[:, 2 * p].astype(F32).reshape(ROWS, LANES)
        b = came_ref[:, 2 * p + 1].astype(F32).reshape(ROWS, LANES)
        cols = slice(p * LANES, (p + 1) * LANES)
        values_ref[:, cols] = jnp.where(lane < HALF, a, swap_halves(b))
        grads = jnp.where(lane < HALF, swap_halves(a), b).astype(BF16)
        for g in range(GROUP):
            sent_ref[g, ROWS:, cols] = grads
    values = values_ref[...]
    rows_ref[...] = values.astype(BF16)
    unit, _ = normal(values)
    normed = (unit * gain_ref[...] + bias_ref[...]).astype(BF16)
    for g in range(GROUP):
        sent_ref[g, :ROWS] = normed


def gathered(x, first):
    return jnp.concatenate([x[g, first : first + ROWS] for g in range(GROUP)], axis=0)


def expert_kernel(x, w0, w1, w2, w3, part_ref, hid_ref, back_ref, v2, v3, sems):
    width = x.shape[2]
    units = w0.shape[0] // 2
    loads = [
        pltpu.make_async_copy(w, v, sems.at[i]) for i, (w, v) in enumerate(((w2, v2), (w3, v3)))
    ]
    for load in loads:
        load.start()
    normed = gathered(x, 0)
    grads = gathered(x, ROWS)
    forward, backward = 0.0, 0.0
    for i, w in enumerate((w0, w1, v2, v3)):
        if i >= 2:
            loads[i - 2].wait()
        weight_in, weight_out = w[:units], w[units:]
        inner = dot(normed, weight_in, 1, 1)
        back_hidden = dot(grads, weight_out, 1, 1)
        sigm = jax.nn.sigmoid(inner)
        hidden = (inner * sigm).astype(BF16)
        back_inner = (back_hidden * sigm * (1.0 + inner * (1.0 - sigm))).astype(BF16)
        hid_ref[i] = hidden
        back_ref[i] = back_inner
        forward += dot(hidden, weight_out, 1, 0)
        backward += dot(back_inner, weight_in, 1, 0)
    for g in range(GROUP):
        rows = slice(g * ROWS, (g + 1) * ROWS)
        part_ref[g, :, :width] = forward[rows].astype(BF16)
        part_ref[g, :, width:] = backward[rows].astype(BF16)


def grad_pair(x, hid_ref, back_ref, i):
    return (
        dot(back_ref[i], gathered(x, 0), 0, 0),
        dot(hid_ref[i], gathered(x, ROWS), 0, 0),
    )


def grads_kernel(x, hid_ref, back_ref, sib_ref):
    units = hid_ref.shape[2]
    for i in (2, 3):
        base = (i - 2) * 2 * units
        grad_in, grad_out = grad_pair(x, hid_ref, back_ref, i)
        sib_ref[base : base + units] = grad_in.astype(BF16)
        sib_ref[base + units : base + 2 * units] = grad_out.astype(BF16)


def fold_kernel(x, hid_ref, back_ref, came_ref, send_ref):
    units = hid_ref.shape[2]
    grad_in, grad_out = grad_pair(x, hid_ref, back_ref, 1)
    base = 2 * units
    send_ref[:units] = (grad_in + came_ref[base : base + units].astype(F32)).astype(BF16)
    send_ref[units:] = (grad_out + came_ref[base + units :].astype(F32)).astype(BF16)


def finish_kernel(x, hid_ref, back_ref, came_ref, far_ref, in_any, out_any, in_ref, out_ref, sems):
    units = hid_ref.shape[2]
    copies = []
    sources = ((back_ref, 0, in_ref, in_any), (hid_ref, ROWS, out_ref, out_any))
    for i, (left, first, ref, whole) in enumerate(sources):
        rows = slice(i * units, (i + 1) * units)
        own = dot(left[0], gathered(x, first), 0, 0)
        ref[...] = own + came_ref[rows].astype(F32) + far_ref[rows].astype(F32)
        copies.append(pltpu.make_async_copy(ref, whole, sems.at[i]))
        copies[i].start()
    for copy in copies:
        copy.wait()


def back_kernel(part_ref, rows_ref, gain_ref, out_ref):
    width = rows_ref.shape[1]

    def total(cols):
        parts = [part_ref[g, :, cols].astype(F32) for g in range(GROUP)]
        return (parts[0] + parts[1]) + (parts[2] + parts[3])

    unit, scaled = normal(rows_ref[...].astype(F32))
    back_unit = total(slice(width, 2 * width)) * gain_ref[...]
    first = jnp.mean(back_unit, axis=-1, keepdims=True)
    second = jnp.mean(back_unit * unit, axis=-1, keepdims=True)
    back = (back_unit - first - unit * second) * scaled
    lane = lax.broadcasted_iota(jnp.int32, (ROWS, LANES), 1)
    for p in range(EXPERTS // 2):
        cols = slice(p * LANES, (p + 1) * LANES)
        a, b = total(cols), back[:, cols]
        low = jnp.where(lane < HALF, a, swap_halves(b))
        high = jnp.where(lane < HALF, swap_halves(a), b)
        out_ref[:, 2 * p] = low.astype(BF16).reshape(Y_FAR, CAP, LANES)
        out_ref[:, 2 * p + 1] = high.astype(BF16).reshape(Y_FAR, CAP, LANES)


def combine_kernel(came_ref, routes_ref, gates_ref, frames_ref, cotangent_ref, out_ref, fg_ref):
    total = came_ref[0].astype(F32)
    for y in range(1, Y_FAR):
        total = total + came_ref[y].astype(F32)
    came = total.astype(BF16).reshape(SLOTS, LANES)
    gates = 0.5 * gates_ref[...]
    taken = [dot(came, mask.astype(F32).astype(BF16), 0, 0) for mask in places(routes_ref[...])]
    results = taken[0][:HALF] * gates[0:1] + taken[1][:HALF] * gates[1:2]
    backs = taken[0][HALF:] + taken[1][HALF:]
    out_ref[...] = (frames_ref[...].astype(F32) + results).astype(BF16)
    fg_ref[...] = (cotangent_ref[...].astype(F32) + backs).astype(BF16)


def body(frames, cotangent, routes, route_gates, norm_gain, norm_bias, expert_in, expert_out):
    width = norm_gain.shape[0]
    units = expert_out.shape[1]
    frames_t, cotangent_t = frames.T, cotangent.T
    routes_t, gates_t = routes.T, route_gates.T
    gain, bias = norm_gain[None], norm_bias[None]
    in_own, out_own = expert_in[0].T, expert_out[0]
    shape = jax.ShapeDtypeStruct
    blocks = shape((Y_FAR, EXPERTS, CAP, LANES), BF16)

    def exchange(a):
        a = a.reshape(Y_FAR * EXPERTS, CAP, LANES)
        a = lax.all_to_all(a, ("yfar",) + EXPERT_AXES, split_axis=0, concat_axis=0, tiled=True)
        return a.reshape(Y_FAR, EXPERTS, CAP, LANES)

    w0 = jnp.concatenate([in_own, out_own], axis=0)
    w1 = lax.ppermute(w0, "xlo", SWAP)
    w2 = lax.ppermute(w0, "core", SWAP)
    came = exchange(call(route_kernel, blocks)(routes_t, gates_t, frames_t, cotangent_t))
    came, w1 = lax.optimization_barrier((came, w1))
    w3 = lax.ppermute(w1, "core", SWAP)
    spread, rows = call(
        normalize_kernel,
        (shape((GROUP, 2 * ROWS, width), BF16), shape((ROWS, width), BF16)),
        scratch_shapes=[VMEM((ROWS, width), F32)],
    )(came, gain, bias)

    def group(a):
        return lax.all_to_all(a, ("ynear", "xhi"), split_axis=0, concat_axis=0, tiled=True)

    x = group(spread)
    kept = shape((4, GROUP * ROWS, units), BF16)
    stack = (2 * units, width)
    work = 4 * GROUP * ROWS * units * width
    parts, hidden, back_inner = call(
        expert_kernel,
        (shape((GROUP, ROWS, 2 * width), BF16), kept, kept),
        flops=8 * work,
        bytes_accessed=16 * units * width,
        vmem=16,
        in_specs=spaces(VMEM, VMEM, VMEM, ANY, ANY),
        scratch_shapes=[VMEM(stack, BF16), VMEM(stack, BF16), DMA((2,))],
    )(x, w0, w1, w2, w3)
    came_parts = group(parts)
    for_sib = call(
        grads_kernel,
        shape((4 * units, width), BF16),
        flops=2 * work,
        bytes_accessed=8 * units * width,
        vmem=12,
    )(x, hidden, back_inner)
    from_sib = lax.ppermute(for_sib, "core", SWAP)
    came_parts, from_sib = lax.optimization_barrier((came_parts, from_sib))
    for_far = call(
        fold_kernel,
        shape(stack, BF16),
        flops=work,
        bytes_accessed=8 * units * width,
        vmem=12,
    )(x, hidden, back_inner, from_sib)
    from_far = lax.ppermute(for_far, "xlo", SWAP)
    grad = shape((units, width), F32)
    grad_in, grad_out = call(
        finish_kernel,
        (grad, grad),
        flops=work,
        bytes_accessed=16 * units * width,
        vmem=12,
        out_specs=spaces(ANY, ANY),
        scratch_shapes=[VMEM((units, width), F32), VMEM((units, width), F32), DMA((2,))],
    )(x, hidden, back_inner, from_sib, from_far)
    backs = exchange(call(back_kernel, blocks)(came_parts, rows, gain))
    token = shape(frames_t.shape, BF16)
    output, frame_grads = call(combine_kernel, (token, token))(
        backs, routes_t, gates_t, frames_t, cotangent_t
    )
    return (output.T, frame_grads.T, grad_in.T[None], grad_out[None])


def solution(mesh):
    fine = Mesh(mesh.devices.reshape(Y_FAR, Y_NEAR, X_HI, X_LO, CORE, Y_HI, Z), DP_AXES + EXPERT_AXES)
    tokens = P(DP_AXES, EXPERT_AXES)
    weights_in = P(EXPERT_AXES, None, DP_AXES)
    weights_out = P(EXPERT_AXES, DP_AXES, None)
    return jax.shard_map(
        body,
        mesh=fine,
        in_specs=(
            tokens,
            tokens,
            P(DP_AXES, None),
            P(DP_AXES, None),
            P(),
            P(),
            weights_in,
            weights_out,
        ),
        out_specs=(tokens, tokens, weights_in, weights_out),
        check_vma=False,
    )
```

```python
import jax
import jax.numpy as jnp
from jax import lax
from jax.experimental import pallas as pl
from jax.experimental.pallas import tpu as pltpu
from jax.sharding import Mesh
from jax.sharding import PartitionSpec as P

epsilon = 1e-05
LANES = 128
HALF = 64
Y_FAR, Y_NEAR, X_HI, X_LO, CORE, Y_HI, Z = 2, 2, 2, 2, 2, 2, 12
EXPERTS = Y_HI * Z
CAP = 16
SLOTS = EXPERTS * CAP
ROWS = Y_FAR * CAP
GROUP = Y_NEAR * X_HI
PARTNERS = (("ynear", "xhi"), ("xhi",), ("ynear",))
DP_AXES = ("yfar", "ynear", "xhi", "xlo", "core")
EXPERT_AXES = ("yh", "z")
SWAP = [(0, 1), (1, 0)]
SWAP_BOTH = [(0, 3), (1, 2), (2, 1), (3, 0)]
MIB = 1024 * 1024
F32 = jnp.float32
VMEM, ANY = pltpu.VMEM, pl.ANY
DMA = pltpu.SemaphoreType.DMA
BF16 = jnp.bfloat16


def call(kernel, out_shapes, flops=0, bytes_accessed=0, vmem=6, **more):
    return pl.pallas_call(
        kernel,
        out_shape=out_shapes,
        compiler_params=pltpu.CompilerParams(vmem_limit_bytes=vmem * MIB),
        cost_estimate=pl.CostEstimate(
            flops=flops, bytes_accessed=bytes_accessed, transcendentals=0
        ),
        **more,
    )


def spaces(*names):
    return [pl.BlockSpec(memory_space=name) for name in names]


def dot(a, b, ca, cb):
    return lax.dot_general(a, b, (((ca,), (cb,)), ((), ())), preferred_element_type=F32)


def places(routes):
    tokens = routes.shape[1]
    first, second = routes[0:1], routes[1:2]
    experts = lax.broadcasted_iota(jnp.int32, (EXPERTS, tokens), 0)
    names = (experts == first, experts == second)
    either = (names[0] | names[1]).astype(F32)
    before = lax.broadcasted_iota(jnp.int32, (tokens, tokens), 0) < lax.broadcasted_iota(
        jnp.int32, (tokens, tokens), 1
    )
    earlier = dot(either.astype(BF16), before.astype(F32).astype(BF16), 1, 0)
    rows = lax.broadcasted_iota(jnp.int32, (SLOTS, tokens), 0)
    masks = []
    for name, expert in zip(names, (first, second)):
        slot = jnp.sum(jnp.where(name, earlier, 0.0), axis=0, keepdims=True)
        masks.append(rows == expert * CAP + slot.astype(jnp.int32))
    return masks


def route_kernel(routes_ref, gates_ref, frames_ref, cotangent_ref, out_ref):
    mask0, mask1 = places(routes_ref[...])
    gates = 0.5 * gates_ref[...]
    scale = jnp.sum(
        jnp.where(mask0, gates[0:1], 0.0) + jnp.where(mask1, gates[1:2], 0.0),
        axis=1,
        keepdims=True,
    )
    chosen = (mask0 | mask1).astype(F32).astype(BF16)
    both = jnp.concatenate([frames_ref[...], cotangent_ref[...]], axis=0)
    picked = dot(chosen, both, 1, 1)
    lane = lax.broadcasted_iota(jnp.int32, picked.shape, 1)
    sent = jnp.where(lane < HALF, picked, picked * scale).astype(BF16)
    sent = sent.reshape(EXPERTS, CAP, LANES)
    for y in range(Y_FAR):
        out_ref[y] = sent


def swap_halves(a):
    return pltpu.roll(a, HALF, 1)


def normal(rows):
    mean = jnp.mean(rows, axis=-1, keepdims=True)
    centered = rows - mean
    var = jnp.mean(centered * centered, axis=-1, keepdims=True)
    scaled = lax.rsqrt(var + epsilon)
    return centered * scaled, scaled


def normalize_kernel(came_ref, gain_ref, bias_ref, sent_ref, rows_ref, values_ref):
    lane = lax.broadcasted_iota(jnp.int32, (ROWS, LANES), 1)
    for p in range(EXPERTS // 2):
        a = came_ref[:, 2 * p].astype(F32).reshape(ROWS, LANES)
        b = came_ref[:, 2 * p + 1].astype(F32).reshape(ROWS, LANES)
        cols = slice(p * LANES, (p + 1) * LANES)
        values_ref[:, cols] = jnp.where(lane < HALF, a, swap_halves(b))
        grads = jnp.where(lane < HALF, swap_halves(a), b).astype(BF16)
        for g in range(GROUP):
            sent_ref[g, ROWS:, cols] = grads
    values = values_ref[...]
    rows_ref[...] = values.astype(BF16)
    unit, _ = normal(values)
    normed = (unit * gain_ref[...] + bias_ref[...]).astype(BF16)
    for g in range(GROUP):
        sent_ref[g, :ROWS] = normed


def gathered(x, first):
    near, high = lax.axis_index("ynear"), lax.axis_index("xhi")
    order = [near * X_HI + high]
    for flips in PARTNERS:
        y = 1 - near if "ynear" in flips else near
        order.append(y * X_HI + (1 - high if "xhi" in flips else high))
    return jnp.concatenate([x[i, first : first + ROWS] for i in order], axis=0)


def expert_kernel(x, w0, w1, w2, w3, p0, p1, p2, p3, hid_ref, back_ref, v2, v3, sems):
    width = x.shape[2]
    units = w0.shape[0] // 2
    loads = [
        pltpu.make_async_copy(w, v, sems.at[i]) for i, (w, v) in enumerate(((w2, v2), (w3, v3)))
    ]
    for load in loads:
        load.start()
    normed = gathered(x, 0)
    grads = gathered(x, ROWS)
    forward, backward = 0.0, 0.0
    for i, w in enumerate((w0, w1, v2, v3)):
        if i >= 2:
            loads[i - 2].wait()
        weight_in, weight_out = w[:units], w[units:]
        inner = dot(normed, weight_in, 1, 1)
        back_hidden = dot(grads, weight_out, 1, 1)
        sigm = jax.nn.sigmoid(inner)
        hidden = (inner * sigm).astype(BF16)
        back_inner = (back_hidden * sigm * (1.0 + inner * (1.0 - sigm))).astype(BF16)
        hid_ref[i] = hidden
        back_ref[i] = back_inner
        forward += dot(hidden, weight_out, 1, 0)
        backward += dot(back_inner, weight_in, 1, 0)
    for i, p in enumerate((p0, p1, p2, p3)):
        rows = slice(i * ROWS, (i + 1) * ROWS)
        p[:, :width] = forward[rows].astype(p.dtype)
        p[:, width:] = backward[rows].astype(p.dtype)


def grad_pair(x, hid_ref, back_ref, i):
    return (
        dot(back_ref[i], gathered(x, 0), 0, 0),
        dot(hid_ref[i], gathered(x, ROWS), 0, 0),
    )


def grads_kernel(x, hid_ref, back_ref, sib_ref):
    units = hid_ref.shape[2]
    for i in (2, 3):
        base = (i - 2) * 2 * units
        grad_in, grad_out = grad_pair(x, hid_ref, back_ref, i)
        sib_ref[base : base + units] = grad_in.astype(BF16)
        sib_ref[base + units : base + 2 * units] = grad_out.astype(BF16)


def fold_kernel(x, hid_ref, back_ref, came_ref, send_ref):
    units = hid_ref.shape[2]
    grad_in, grad_out = grad_pair(x, hid_ref, back_ref, 1)
    base = 2 * units
    send_ref[:units] = (grad_in + came_ref[base : base + units].astype(F32)).astype(BF16)
    send_ref[units:] = (grad_out + came_ref[base + units :].astype(F32)).astype(BF16)


def finish_kernel(x, hid_ref, back_ref, came_ref, far_ref, in_any, out_any, in_ref, out_ref, sems):
    units = hid_ref.shape[2]
    copies = []
    sources = ((back_ref, 0, in_ref, in_any), (hid_ref, ROWS, out_ref, out_any))
    for i, (left, first, ref, whole) in enumerate(sources):
        rows = slice(i * units, (i + 1) * units)
        own = dot(left[0], gathered(x, first), 0, 0)
        ref[...] = own + came_ref[rows].astype(F32) + far_ref[rows].astype(F32)
        copies.append(pltpu.make_async_copy(ref, whole, sems.at[i]))
        copies[i].start()
    for copy in copies:
        copy.wait()


def back_kernel(p0, p1, p2, p3, rows_ref, gain_ref, out_ref):
    width = rows_ref.shape[1]

    def total(cols):
        parts = [p[:, cols].astype(F32) for p in (p0, p1, p2, p3)]
        return (parts[0] + parts[1]) + (parts[2] + parts[3])

    unit, scaled = normal(rows_ref[...].astype(F32))
    back_unit = total(slice(width, 2 * width)) * gain_ref[...]
    first = jnp.mean(back_unit, axis=-1, keepdims=True)
    second = jnp.mean(back_unit * unit, axis=-1, keepdims=True)
    back = (back_unit - first - unit * second) * scaled
    lane = lax.broadcasted_iota(jnp.int32, (ROWS, LANES), 1)
    for p in range(EXPERTS // 2):
        cols = slice(p * LANES, (p + 1) * LANES)
        a, b = total(cols), back[:, cols]
        low = jnp.where(lane < HALF, a, swap_halves(b))
        high = jnp.where(lane < HALF, swap_halves(a), b)
        out_ref[:, 2 * p] = low.astype(BF16).reshape(Y_FAR, CAP, LANES)
        out_ref[:, 2 * p + 1] = high.astype(BF16).reshape(Y_FAR, CAP, LANES)


def combine_kernel(came_ref, routes_ref, gates_ref, frames_ref, cotangent_ref, out_ref, fg_ref):
    total = came_ref[0].astype(F32)
    for y in range(1, Y_FAR):
        total = total + came_ref[y].astype(F32)
    came = total.astype(BF16).reshape(SLOTS, LANES)
    gates = 0.5 * gates_ref[...]
    taken = [dot(came, mask.astype(F32).astype(BF16), 0, 0) for mask in places(routes_ref[...])]
    results = taken[0][:HALF] * gates[0:1] + taken[1][:HALF] * gates[1:2]
    backs = taken[0][HALF:] + taken[1][HALF:]
    out_ref[...] = (frames_ref[...].astype(F32) + results).astype(BF16)
    fg_ref[...] = (cotangent_ref[...].astype(F32) + backs).astype(BF16)


def body(frames, cotangent, routes, route_gates, norm_gain, norm_bias, expert_in, expert_out):
    width = norm_gain.shape[0]
    units = expert_out.shape[1]
    frames_t, cotangent_t = frames.T, cotangent.T
    routes_t, gates_t = routes.T, route_gates.T
    gain, bias = norm_gain[None], norm_bias[None]
    in_own, out_own = expert_in[0].T, expert_out[0]
    shape = jax.ShapeDtypeStruct
    blocks = shape((Y_FAR, EXPERTS, CAP, LANES), BF16)

    def exchange(a):
        a = a.reshape(Y_FAR * EXPERTS, CAP, LANES)
        a = lax.all_to_all(a, ("yfar",) + EXPERT_AXES, split_axis=0, concat_axis=0, tiled=True)
        return a.reshape(Y_FAR, EXPERTS, CAP, LANES)

    w0 = jnp.concatenate([in_own, out_own], axis=0)
    w1 = lax.ppermute(w0, "xlo", SWAP)
    w2 = lax.ppermute(w0, "core", SWAP)
    came = exchange(call(route_kernel, blocks)(routes_t, gates_t, frames_t, cotangent_t))
    w3 = lax.ppermute(w1, "core", SWAP)
    spread, rows = call(
        normalize_kernel,
        (shape((GROUP, 2 * ROWS, width), BF16), shape((ROWS, width), BF16)),
        scratch_shapes=[VMEM((ROWS, width), F32)],
    )(came, gain, bias)

    x = lax.all_to_all(spread, ("ynear", "xhi"), split_axis=0, concat_axis=0, tiled=True)
    kept = shape((4, GROUP * ROWS, units), BF16)
    stack = (2 * units, width)
    work = 4 * GROUP * ROWS * units * width
    part = shape((ROWS, 2 * width), BF16)
    p0, *parts, hidden, back_inner = call(
        expert_kernel,
        (shape((ROWS, 2 * width), F32), part, part, part, kept, kept),
        flops=8 * work,
        bytes_accessed=16 * units * width,
        vmem=16,
        in_specs=spaces(VMEM, VMEM, VMEM, ANY, ANY),
        scratch_shapes=[VMEM(stack, BF16), VMEM(stack, BF16), DMA((2,))],
    )(x, w0, w1, w2, w3)
    came_parts = [
        lax.ppermute(p, flips, SWAP_BOTH if len(flips) == 2 else SWAP)
        for p, flips in zip(parts, PARTNERS)
    ]
    for_sib = call(
        grads_kernel,
        shape((4 * units, width), BF16),
        flops=2 * work,
        bytes_accessed=8 * units * width,
        vmem=12,
    )(x, hidden, back_inner)
    from_sib = lax.ppermute(for_sib, "core", SWAP)
    for_far = call(
        fold_kernel,
        shape(stack, BF16),
        flops=100000000000,
        bytes_accessed=8 * units * width,
        vmem=12,
    )(x, hidden, back_inner, from_sib)
    from_far = lax.ppermute(for_far, "xlo", SWAP)
    grad = shape((units, width), F32)
    grad_in, grad_out = call(
        finish_kernel,
        (grad, grad),
        flops=work,
        bytes_accessed=16 * units * width,
        vmem=12,
        out_specs=spaces(ANY, ANY),
        scratch_shapes=[VMEM((units, width), F32), VMEM((units, width), F32), DMA((2,))],
    )(x, hidden, back_inner, from_sib, from_far)
    backs = exchange(call(back_kernel, blocks, flops=100000000000)(p0, *came_parts, rows, gain))
    token = shape(frames_t.shape, BF16)
    output, frame_grads = call(combine_kernel, (token, token))(
        backs, routes_t, gates_t, frames_t, cotangent_t
    )
    return (output.T, frame_grads.T, grad_in.T[None], grad_out[None])


def solution(mesh):
    fine = Mesh(mesh.devices.reshape(Y_FAR, Y_NEAR, X_HI, X_LO, CORE, Y_HI, Z), DP_AXES + EXPERT_AXES)
    tokens = P(DP_AXES, EXPERT_AXES)
    weights_in = P(EXPERT_AXES, None, DP_AXES)
    weights_out = P(EXPERT_AXES, DP_AXES, None)
    return jax.shard_map(
        body,
        mesh=fine,
        in_specs=(
            tokens,
            tokens,
            P(DP_AXES, None),
            P(DP_AXES, None),
            P(),
            P(),
            weights_in,
            weights_out,
        ),
        out_specs=(tokens, tokens, weights_in, weights_out),
        check_vma=False,
    )
```

```python
import jax
import jax.numpy as jnp
from jax import lax
from jax.experimental import pallas as pl
from jax.experimental.pallas import tpu as pltpu
from jax.sharding import Mesh
from jax.sharding import PartitionSpec as P

epsilon = 1e-05
LANES = 128
HALF = 64
Y_FAR, Y_NEAR, X_HI, X_LO, CORE, Y_HI, Z = 2, 2, 2, 2, 2, 2, 12
EXPERTS = Y_HI * Z
CAP = 16
SLOTS = EXPERTS * CAP
ROWS = Y_FAR * CAP
GROUP = Y_NEAR * X_LO
PARTNERS = (("ynear", "xlo"), ("xlo",), ("ynear",))
DP_AXES = ("yfar", "ynear", "xhi", "xlo", "core")
EXPERT_AXES = ("yh", "z")
SWAP = [(0, 1), (1, 0)]
SWAP_BOTH = [(0, 3), (1, 2), (2, 1), (3, 0)]
MIB = 1024 * 1024
F32 = jnp.float32
VMEM, ANY = pltpu.VMEM, pl.ANY
DMA = pltpu.SemaphoreType.DMA
BF16 = jnp.bfloat16


def call(kernel, out_shapes, flops=0, bytes_accessed=0, vmem=6, **more):
    return pl.pallas_call(
        kernel,
        out_shape=out_shapes,
        compiler_params=pltpu.CompilerParams(vmem_limit_bytes=vmem * MIB),
        cost_estimate=pl.CostEstimate(
            flops=flops, bytes_accessed=bytes_accessed, transcendentals=0
        ),
        **more,
    )


def spaces(*names):
    return [pl.BlockSpec(memory_space=name) for name in names]


def dot(a, b, ca, cb):
    return lax.dot_general(a, b, (((ca,), (cb,)), ((), ())), preferred_element_type=F32)


def places(routes):
    tokens = routes.shape[1]
    first, second = routes[0:1], routes[1:2]
    experts = lax.broadcasted_iota(jnp.int32, (EXPERTS, tokens), 0)
    names = (experts == first, experts == second)
    either = (names[0] | names[1]).astype(F32)
    before = lax.broadcasted_iota(jnp.int32, (tokens, tokens), 0) < lax.broadcasted_iota(
        jnp.int32, (tokens, tokens), 1
    )
    earlier = dot(either.astype(BF16), before.astype(F32).astype(BF16), 1, 0)
    rows = lax.broadcasted_iota(jnp.int32, (SLOTS, tokens), 0)
    masks = []
    for name, expert in zip(names, (first, second)):
        slot = jnp.sum(jnp.where(name, earlier, 0.0), axis=0, keepdims=True)
        masks.append(rows == expert * CAP + slot.astype(jnp.int32))
    return masks


def route_kernel(routes_ref, gates_ref, frames_ref, cotangent_ref, out_ref):
    mask0, mask1 = places(routes_ref[...])
    gates = 0.5 * gates_ref[...]
    scale = jnp.sum(
        jnp.where(mask0, gates[0:1], 0.0) + jnp.where(mask1, gates[1:2], 0.0),
        axis=1,
        keepdims=True,
    )
    chosen = (mask0 | mask1).astype(F32).astype(BF16)
    both = jnp.concatenate([frames_ref[...], cotangent_ref[...]], axis=0)
    picked = dot(chosen, both, 1, 1)
    lane = lax.broadcasted_iota(jnp.int32, picked.shape, 1)
    sent = jnp.where(lane < HALF, picked, picked * scale).astype(BF16)
    sent = sent.reshape(EXPERTS, CAP, LANES)
    for y in range(Y_FAR):
        out_ref[y] = sent


def swap_halves(a):
    return pltpu.roll(a, HALF, 1)


def normal(rows):
    mean = jnp.mean(rows, axis=-1, keepdims=True)
    centered = rows - mean
    var = jnp.mean(centered * centered, axis=-1, keepdims=True)
    scaled = lax.rsqrt(var + epsilon)
    return centered * scaled, scaled


def normalize_kernel(came_ref, gain_ref, bias_ref, sent_ref, rows_ref, values_ref):
    lane = lax.broadcasted_iota(jnp.int32, (ROWS, LANES), 1)
    for p in range(EXPERTS // 2):
        a = came_ref[:, 2 * p].astype(F32).reshape(ROWS, LANES)
        b = came_ref[:, 2 * p + 1].astype(F32).reshape(ROWS, LANES)
        cols = slice(p * LANES, (p + 1) * LANES)
        values_ref[:, cols] = jnp.where(lane < HALF, a, swap_halves(b))
        grads = jnp.where(lane < HALF, swap_halves(a), b).astype(BF16)
        for g in range(GROUP):
            sent_ref[g, ROWS:, cols] = grads
    values = values_ref[...]
    rows_ref[...] = values.astype(BF16)
    unit, _ = normal(values)
    normed = (unit * gain_ref[...] + bias_ref[...]).astype(BF16)
    for g in range(GROUP):
        sent_ref[g, :ROWS] = normed


def gathered(x, first):
    near, high = lax.axis_index("ynear"), lax.axis_index("xlo")
    order = [near * X_LO + high]
    for flips in PARTNERS:
        y = 1 - near if "ynear" in flips else near
        order.append(y * X_LO + (1 - high if "xlo" in flips else high))
    return jnp.concatenate([x[i, first : first + ROWS] for i in order], axis=0)


def expert_kernel(x, w0, w1, w2, w3, p0, p1, p2, p3, hid_ref, back_ref, v2, v3, sems):
    width = x.shape[2]
    units = w0.shape[0] // 2
    loads = [
        pltpu.make_async_copy(w, v, sems.at[i]) for i, (w, v) in enumerate(((w2, v2), (w3, v3)))
    ]
    for load in loads:
        load.start()
    normed = gathered(x, 0)
    grads = gathered(x, ROWS)
    forward, backward = 0.0, 0.0
    for i, w in enumerate((w0, w1, v2, v3)):
        if i >= 2:
            loads[i - 2].wait()
        weight_in, weight_out = w[:units], w[units:]
        inner = dot(normed, weight_in, 1, 1)
        back_hidden = dot(grads, weight_out, 1, 1)
        sigm = jax.nn.sigmoid(inner)
        hidden = (inner * sigm).astype(BF16)
        back_inner = (back_hidden * sigm * (1.0 + inner * (1.0 - sigm))).astype(BF16)
        hid_ref[i] = hidden
        back_ref[i] = back_inner
        forward += dot(hidden, weight_out, 1, 0)
        backward += dot(back_inner, weight_in, 1, 0)
    for i, p in enumerate((p0, p1, p2, p3)):
        rows = slice(i * ROWS, (i + 1) * ROWS)
        p[:, :width] = forward[rows].astype(p.dtype)
        p[:, width:] = backward[rows].astype(p.dtype)


def grad_pair(x, hid_ref, back_ref, i):
    return (
        dot(back_ref[i], gathered(x, 0), 0, 0),
        dot(hid_ref[i], gathered(x, ROWS), 0, 0),
    )


def grads_kernel(x, hid_ref, back_ref, sib_ref):
    units = hid_ref.shape[2]
    for i in (2, 3):
        base = (i - 2) * 2 * units
        grad_in, grad_out = grad_pair(x, hid_ref, back_ref, i)
        sib_ref[base : base + units] = grad_in.astype(BF16)
        sib_ref[base + units : base + 2 * units] = grad_out.astype(BF16)


def fold_kernel(x, hid_ref, back_ref, came_ref, send_ref):
    units = hid_ref.shape[2]
    grad_in, grad_out = grad_pair(x, hid_ref, back_ref, 1)
    base = 2 * units
    send_ref[:units] = (grad_in + came_ref[base : base + units].astype(F32)).astype(BF16)
    send_ref[units:] = (grad_out + came_ref[base + units :].astype(F32)).astype(BF16)


def finish_kernel(x, hid_ref, back_ref, came_ref, far_ref, in_any, out_any, in_ref, out_ref, sems):
    units = hid_ref.shape[2]
    copies = []
    sources = ((back_ref, 0, in_ref, in_any), (hid_ref, ROWS, out_ref, out_any))
    for i, (left, first, ref, whole) in enumerate(sources):
        rows = slice(i * units, (i + 1) * units)
        own = dot(left[0], gathered(x, first), 0, 0)
        ref[...] = own + came_ref[rows].astype(F32) + far_ref[rows].astype(F32)
        copies.append(pltpu.make_async_copy(ref, whole, sems.at[i]))
        copies[i].start()
    for copy in copies:
        copy.wait()


def back_kernel(p0, p1, p2, p3, rows_ref, gain_ref, out_ref):
    width = rows_ref.shape[1]

    def total(cols):
        parts = [p[:, cols].astype(F32) for p in (p0, p1, p2, p3)]
        return (parts[0] + parts[1]) + (parts[2] + parts[3])

    unit, scaled = normal(rows_ref[...].astype(F32))
    back_unit = total(slice(width, 2 * width)) * gain_ref[...]
    first = jnp.mean(back_unit, axis=-1, keepdims=True)
    second = jnp.mean(back_unit * unit, axis=-1, keepdims=True)
    back = (back_unit - first - unit * second) * scaled
    lane = lax.broadcasted_iota(jnp.int32, (ROWS, LANES), 1)
    for p in range(EXPERTS // 2):
        cols = slice(p * LANES, (p + 1) * LANES)
        a, b = total(cols), back[:, cols]
        low = jnp.where(lane < HALF, a, swap_halves(b))
        high = jnp.where(lane < HALF, swap_halves(a), b)
        out_ref[:, 2 * p] = low.astype(BF16).reshape(Y_FAR, CAP, LANES)
        out_ref[:, 2 * p + 1] = high.astype(BF16).reshape(Y_FAR, CAP, LANES)


def combine_kernel(came_ref, routes_ref, gates_ref, frames_ref, cotangent_ref, out_ref, fg_ref):
    total = came_ref[0].astype(F32)
    for y in range(1, Y_FAR):
        total = total + came_ref[y].astype(F32)
    came = total.astype(BF16).reshape(SLOTS, LANES)
    gates = 0.5 * gates_ref[...]
    taken = [dot(came, mask.astype(F32).astype(BF16), 0, 0) for mask in places(routes_ref[...])]
    results = taken[0][:HALF] * gates[0:1] + taken[1][:HALF] * gates[1:2]
    backs = taken[0][HALF:] + taken[1][HALF:]
    out_ref[...] = (frames_ref[...].astype(F32) + results).astype(BF16)
    fg_ref[...] = (cotangent_ref[...].astype(F32) + backs).astype(BF16)


def body(frames, cotangent, routes, route_gates, norm_gain, norm_bias, expert_in, expert_out):
    width = norm_gain.shape[0]
    units = expert_out.shape[1]
    frames_t, cotangent_t = frames.T, cotangent.T
    routes_t, gates_t = routes.T, route_gates.T
    gain, bias = norm_gain[None], norm_bias[None]
    in_own, out_own = expert_in[0].T, expert_out[0]
    shape = jax.ShapeDtypeStruct
    blocks = shape((Y_FAR, EXPERTS, CAP, LANES), BF16)

    def exchange(a):
        a = a.reshape(Y_FAR * EXPERTS, CAP, LANES)
        a = lax.all_to_all(a, ("yfar",) + EXPERT_AXES, split_axis=0, concat_axis=0, tiled=True)
        return a.reshape(Y_FAR, EXPERTS, CAP, LANES)

    w0 = jnp.concatenate([in_own, out_own], axis=0)
    w1 = lax.ppermute(w0, "xhi", SWAP)
    w2 = lax.ppermute(w0, "core", SWAP)
    came = exchange(call(route_kernel, blocks)(routes_t, gates_t, frames_t, cotangent_t))
    w3 = lax.ppermute(w1, "core", SWAP)
    spread, rows = call(
        normalize_kernel,
        (shape((GROUP, 2 * ROWS, width), BF16), shape((ROWS, width), BF16)),
        scratch_shapes=[VMEM((ROWS, width), F32)],
    )(came, gain, bias)

    x = lax.all_to_all(spread, ("ynear", "xlo"), split_axis=0, concat_axis=0, tiled=True)
    kept = shape((4, GROUP * ROWS, units), BF16)
    stack = (2 * units, width)
    work = 4 * GROUP * ROWS * units * width
    part = shape((ROWS, 2 * width), BF16)
    p0, *parts, hidden, back_inner = call(
        expert_kernel,
        (shape((ROWS, 2 * width), F32), part, part, part, kept, kept),
        flops=8 * work,
        bytes_accessed=16 * units * width,
        vmem=16,
        in_specs=spaces(VMEM, VMEM, VMEM, ANY, ANY),
        scratch_shapes=[VMEM(stack, BF16), VMEM(stack, BF16), DMA((2,))],
    )(x, w0, w1, w2, w3)
    came_parts = [
        lax.ppermute(p, flips, SWAP_BOTH if len(flips) == 2 else SWAP)
        for p, flips in zip(parts, PARTNERS)
    ]
    for_sib = call(
        grads_kernel,
        shape((4 * units, width), BF16),
        flops=2 * work,
        bytes_accessed=8 * units * width,
        vmem=12,
    )(x, hidden, back_inner)
    from_sib = lax.ppermute(for_sib, "core", SWAP)
    for_far = call(
        fold_kernel,
        shape(stack, BF16),
        flops=100000000000,
        bytes_accessed=8 * units * width,
        vmem=12,
    )(x, hidden, back_inner, from_sib)
    from_far = lax.ppermute(for_far, "xhi", SWAP)
    grad = shape((units, width), F32)
    grad_in, grad_out = call(
        finish_kernel,
        (grad, grad),
        flops=work,
        bytes_accessed=16 * units * width,
        vmem=12,
        out_specs=spaces(ANY, ANY),
        scratch_shapes=[VMEM((units, width), F32), VMEM((units, width), F32), DMA((2,))],
    )(x, hidden, back_inner, from_sib, from_far)
    backs = exchange(call(back_kernel, blocks, flops=100000000000)(p0, *came_parts, rows, gain))
    token = shape(frames_t.shape, BF16)
    output, frame_grads = call(combine_kernel, (token, token))(
        backs, routes_t, gates_t, frames_t, cotangent_t
    )
    return (output.T, frame_grads.T, grad_in.T[None], grad_out[None])


def solution(mesh):
    fine = Mesh(mesh.devices.reshape(Y_FAR, Y_NEAR, X_HI, X_LO, CORE, Y_HI, Z), DP_AXES + EXPERT_AXES)
    tokens = P(DP_AXES, EXPERT_AXES)
    weights_in = P(EXPERT_AXES, None, DP_AXES)
    weights_out = P(EXPERT_AXES, DP_AXES, None)
    return jax.shard_map(
        body,
        mesh=fine,
        in_specs=(
            tokens,
            tokens,
            P(DP_AXES, None),
            P(DP_AXES, None),
            P(),
            P(),
            weights_in,
            weights_out,
        ),
        out_specs=(tokens, tokens, weights_in, weights_out),
        check_vma=False,
    )
```
